256 devices in a mesh: section: 8 (over x, core), ctx: 32 (over z, y).
Axes of the slice: x: 4, y: 4, z: 8, core: 2. Of those that a mesh axis runs over, the one named last changes fastest.
Arguments:
- queries: bfloat16 [8, 8192, 2560], P('section', 'ctx'), may hold values from -6 to 6
- keys: bfloat16 [8, 8192, 512], P('section', 'ctx'), may hold values from -6 to 6
- values: bfloat16 [8, 8192, 512], P('section', 'ctx'), may hold values from -6 to 6
- outputs: bfloat16 [8, 8192, 2560], P('section', 'ctx'), may hold values from -3 to 3
- grad_out: bfloat16 [8, 8192, 2560], P('section', 'ctx'), may hold values from -3 to 3
- log_sums: float32 [8, 20, 8192], P('section', None, 'ctx'), may hold values from 2 to 4
- doc_lengths: int32 [8, 64], P('section'), may hold values from 1 to 768, 8192 in all within a row
Outputs:
- grad_queries: bfloat16 [8, 8192, 2560], P('section', 'ctx')
- grad_keys: bfloat16 [8, 8192, 512], P('section', 'ctx')
- grad_values: bfloat16 [8, 8192, 512], P('section', 'ctx')
The draws below stay inside these ranges and needn't reach their ends.
Inputs may be any that keep to these rules, and one draw needn't show every extreme that they name: `doc_lengths`: each row lists one section's documents in order; a row sums to 8192 and its longest document has exactly 768 tokens.
All inputs are finite; a program needn't handle non-finite values.
Results may differ from the reference program's by a relative error of at most 0.0059.
Values may be sent and summed in bfloat16 or wider, within the bound.
No kernel may reach another device: no remote copies, remote signals or barrier semaphores. Data moves between devices by JAX's collectives and lax.ppermute only.
A program may use at most 64 MiB of HBM per device.

```python
import math
import jax
import jax.numpy as jnp
import numpy as np
from jax import lax

QUERY_HEADS = 20
KEY_VALUE_HEADS = 4
HEAD_WIDTH = 128
BLK = 128
CASCADE_PARTS = 8
PACKED_TOKENS = 8192
DOCS = 64
LONGEST_TOKENS = 768


def level_of(key, extent, split, smallest, top_value):
    def one(position, parts):
        heights = jax.random.uniform(jax.random.fold_in(jax.random.fold_in(key, 6), position), (parts,), jnp.float32, smallest / len(split), top_value / len(split))
        return jnp.repeat(jnp.exp(heights), extent[position] // parts).reshape((-1,) + (1,) * (len(extent) - position - 1))

    level = one(*split[0])
    for cut in split[1:]:
        level = level * one(*cut)
    return level


def length_profile(amount, total, limit, slope):
    weights = [(1 << 20) // math.isqrt(rank ** slope) + 1 for rank in range(2, amount + 1)]
    spare, holding = total - limit - (amount - 1), [1] * (amount - 1)
    while spare > 0:
        free = [i for i in range(amount - 1) if holding[i] < limit]
        whole, left = sum([weights[i] for i in free]), spare
        for i in free:
            addition = min(limit - holding[i], max(1, left * weights[i] // whole), spare)
            holding[i] = holding[i] + addition
            spare = spare - addition
    return np.array([limit] + holding)


def ragged(own_key, count, total, bound, lean):
    if count == 2:
        one = jax.random.randint(own_key, (), max(1, total - bound), min(bound, total - 1) + 1)
        return jnp.stack([one, total - one])
    tallies = jnp.asarray(length_profile(count, total, bound, lean), jnp.int32)
    twos = (count - 1) // 2
    donor, sink = tallies[1:1 + 2 * twos:2], tallies[2:2 + 2 * twos:2]
    slack = jnp.minimum(donor - 1, bound - sink)
    passed = jax.random.randint(jax.random.fold_in(own_key, 1), (twos,), 0, 1 << 20) % (slack + 1)
    tallies = tallies.at[1:1 + 2 * twos:2].set(donor - passed).at[2:2 + 2 * twos:2].set(sink + passed)
    return tallies[jax.random.permutation(jax.random.fold_in(own_key, 2), count)]


def centred(key, extent, scale, bound, shards=(), kind=jnp.bfloat16):
    result = scale * jax.random.normal(key, extent, jnp.float32)
    if shards:
        result = result * level_of(key, extent, shards, -0.22, 0.18)
    return jnp.clip(result, -bound, bound).astype(kind)


def setup_inputs(seed: int = 0) -> dict:
    splits = jax.random.split(jax.random.key(seed), 8)
    queries = centred(splits[0], (CASCADE_PARTS, PACKED_TOKENS, QUERY_HEADS * HEAD_WIDTH), 1.0, 6.0, ((0, 8), (1, 32)))
    keys = centred(splits[1], (CASCADE_PARTS, PACKED_TOKENS, KEY_VALUE_HEADS * HEAD_WIDTH), 1.0, 6.0, ((0, 8), (1, 32)))
    values = centred(splits[2], (CASCADE_PARTS, PACKED_TOKENS, KEY_VALUE_HEADS * HEAD_WIDTH), 1.0, 6.0, ((0, 8), (1, 32)))
    outputs = centred(splits[3], (CASCADE_PARTS, PACKED_TOKENS, QUERY_HEADS * HEAD_WIDTH), 0.5, 3.0, ((0, 8), (1, 32)))
    grad_out = centred(splits[4], (CASCADE_PARTS, PACKED_TOKENS, QUERY_HEADS * HEAD_WIDTH), 0.5, 3.0, ((0, 8), (1, 32)))
    log_sums = jnp.clip(2.0 + 2.0 * jax.random.uniform(splits[5], (CASCADE_PARTS, QUERY_HEADS, PACKED_TOKENS), jnp.float32) ** level_of(splits[5], (CASCADE_PARTS, QUERY_HEADS, PACKED_TOKENS), ((0, 8), (2, 32)), -0.2, 0.2), 2.0, 4.0)
    doc_lengths = jax.vmap(lambda own: ragged(own, DOCS, PACKED_TOKENS, LONGEST_TOKENS, 2))(jax.random.split(splits[6], CASCADE_PARTS)).reshape((CASCADE_PARTS, DOCS)).astype(jnp.int32)
    return dict(queries=queries, keys=keys, values=values, outputs=outputs, grad_out=grad_out, log_sums=log_sums, doc_lengths=doc_lengths)


def segment_of(positions, doc_ends):
    counted = jnp.sum((doc_ends[None, :] <= positions[:, None]).astype(jnp.int32), axis=1).astype(jnp.int32)
    return jnp.where(positions < 0, -1, counted).astype(jnp.int32)


def attention_grads(query_row_block, output_grad_rows, logsum_rows, delta_by_row, key_row_block, value_row_block, allowed):
    softmax_scale = HEAD_WIDTH ** -0.5
    group_width = QUERY_HEADS // KEY_VALUE_HEADS
    query_total_count = query_row_block.shape[0]
    key_total_count = key_row_block.shape[0]
    heads_of_queries = query_row_block.astype(jnp.float32).reshape(query_total_count, KEY_VALUE_HEADS, group_width, HEAD_WIDTH)
    cotangent_by_head = output_grad_rows.astype(jnp.float32).reshape(query_total_count, KEY_VALUE_HEADS, group_width, HEAD_WIDTH)
    heads_of_keys = key_row_block.astype(jnp.float32).reshape(key_total_count, KEY_VALUE_HEADS, HEAD_WIDTH)
    heads_of_values = value_row_block.astype(jnp.float32).reshape(key_total_count, KEY_VALUE_HEADS, HEAD_WIDTH)
    scores = jnp.einsum("qhgd,khd->hgqk", heads_of_queries, heads_of_keys) * softmax_scale
    logsum_matrix = logsum_rows.reshape(KEY_VALUE_HEADS, group_width, query_total_count)
    delta_matrix = delta_by_row.reshape(KEY_VALUE_HEADS, group_width, query_total_count)
    weights = jnp.where(allowed[None, None], jnp.exp(scores - logsum_matrix[..., None]), 0.0)
    weight_lowprec = lax.optimization_barrier(weights.astype(jnp.bfloat16))
    weight_grads = jnp.einsum("qhgd,khd->hgqk", cotangent_by_head, heads_of_values)
    dscore = lax.optimization_barrier((weights * (weight_grads - delta_matrix[..., None])).astype(jnp.bfloat16))
    score_grad_full = dscore.astype(jnp.float32)
    grad_q = jnp.einsum("hgqk,khd->qhgd", score_grad_full, heads_of_keys).reshape(query_total_count, QUERY_HEADS * HEAD_WIDTH) * softmax_scale
    key_gradient = jnp.einsum("iuvw,viul->wil", score_grad_full, heads_of_queries).reshape(key_total_count, KEY_VALUE_HEADS * HEAD_WIDTH) * softmax_scale
    value_gradient = jnp.einsum("iuvw,viul->wil", weight_lowprec.astype(jnp.float32), cotangent_by_head).reshape(key_total_count, KEY_VALUE_HEADS * HEAD_WIDTH)
    return grad_q, key_gradient, value_gradient


def section_grads(section_inputs):
    queries, keys, values, outputs, grad_out, log_sums, doc_lengths = section_inputs
    token_list = queries.shape[0]
    doc_ends = jnp.cumsum(doc_lengths).astype(jnp.int32)
    segments = segment_of(jnp.arange(token_list, dtype=jnp.int32), doc_ends)
    delta_all = jnp.sum((grad_out.astype(jnp.float32) * outputs.astype(jnp.float32)).reshape(token_list, QUERY_HEADS, HEAD_WIDTH), axis=2).T
    window_rows = LONGEST_TOKENS + BLK
    keys_padded_out = jnp.concatenate([jnp.zeros((LONGEST_TOKENS, KEY_VALUE_HEADS * HEAD_WIDTH), keys.dtype), keys], axis=0)
    values_padded_out = jnp.concatenate([jnp.zeros((LONGEST_TOKENS, KEY_VALUE_HEADS * HEAD_WIDTH), values.dtype), values], axis=0)
    padded_segments = jnp.concatenate([-jnp.ones((LONGEST_TOKENS,), jnp.int32), segments], axis=0)

    def advance(carry_pair, block_index):
        keys_total, values_total = carry_pair
        start_row = (block_index * BLK).astype(jnp.int32)
        query_row_block = lax.dynamic_slice_in_dim(queries, start_row, BLK, 0)
        output_grad_rows = lax.dynamic_slice_in_dim(grad_out, start_row, BLK, 0)
        logsum_rows = lax.dynamic_slice_in_dim(log_sums, start_row, BLK, 1)
        delta_by_row = lax.dynamic_slice_in_dim(delta_all, start_row, BLK, 1)
        key_row_block = lax.dynamic_slice_in_dim(keys_padded_out, start_row, window_rows, 0)
        value_row_block = lax.dynamic_slice_in_dim(values_padded_out, start_row, window_rows, 0)
        key_segments = lax.dynamic_slice_in_dim(padded_segments, start_row, window_rows, 0)
        query_segments = lax.dynamic_slice_in_dim(segments, start_row, BLK, 0)
        query_pos = start_row + jnp.arange(BLK, dtype=jnp.int32)
        key_pos = start_row - LONGEST_TOKENS + jnp.arange(window_rows, dtype=jnp.int32)
        allowed = (query_segments[:, None] == key_segments[None, :]) & (key_pos[None, :] <= query_pos[:, None])
        grad_q, key_gradient, value_gradient = attention_grads(query_row_block, output_grad_rows, logsum_rows, delta_by_row, key_row_block, value_row_block, allowed)
        keys_total = lax.dynamic_update_slice_in_dim(keys_total, lax.dynamic_slice_in_dim(keys_total, start_row, window_rows, 0) + key_gradient, start_row, 0)
        values_total = lax.dynamic_update_slice_in_dim(values_total, lax.dynamic_slice_in_dim(values_total, start_row, window_rows, 0) + value_gradient, start_row, 0)
        return (keys_total, values_total), grad_q

    blank_buffer = jnp.zeros((token_list + LONGEST_TOKENS, KEY_VALUE_HEADS * HEAD_WIDTH), jnp.float32)
    totals, grad_q = lax.scan(advance, (blank_buffer, blank_buffer), jnp.arange(token_list // BLK, dtype=jnp.int32))
    return grad_q.reshape(token_list, QUERY_HEADS * HEAD_WIDTH), totals[0][LONGEST_TOKENS:], totals[1][LONGEST_TOKENS:]


def reference(queries, keys, values, outputs, grad_out, log_sums, doc_lengths):
    grad_q, key_gradient, value_gradient = lax.map(section_grads, (queries, keys, values, outputs, grad_out, log_sums, doc_lengths))
    return (jnp.roll(grad_q, -1, axis=0).astype(jnp.bfloat16),
            jnp.roll(key_gradient, -1, axis=0).astype(jnp.bfloat16),
            jnp.roll(value_gradient, -1, axis=0).astype(jnp.bfloat16))
```

```python
import functools
import math

import jax
import jax.numpy as jnp
from jax import lax
from jax.experimental import pallas as pl
from jax.experimental.pallas import tpu as pltpu
from jax.sharding import PartitionSpec as P

QUERY_HEADS = 20
KEY_VALUE_HEADS = 4
GROUP = QUERY_HEADS // KEY_VALUE_HEADS
WIDTH = 128
SCALE = WIDTH ** (-0.5)
LOG2E = math.log2(math.e)
MASKED = -1e30
NT = (((1,), (1,)), ((), ()))
NN = (((1,), (0,)), ((), ()))


def around(x, axis, by):
    peers = lax.axis_size(axis)
    return lax.ppermute(x, axis, [(i, (i + by) % peers) for i in range(peers)])


def dot(a, b, dims):
    return lax.dot_general(a, b, dims, preferred_element_type=jnp.float32)


def first_token(lengths, query_pos):
    docs = lengths.shape[1]
    row = lax.broadcasted_iota(jnp.int32, (docs, docs), 0)
    col = lax.broadcasted_iota(jnp.int32, (docs, docs), 1)
    ends = jnp.sum(jnp.where(col <= row, lengths, 0), axis=1, keepdims=True)
    return jnp.max(jnp.where(ends <= query_pos, ends, 0), axis=0, keepdims=True)


def block_bias(start, rows, base_key, base_query):
    key_pos = base_key + lax.broadcasted_iota(jnp.int32, (rows, rows), 0)
    query_pos = base_query + lax.broadcasted_iota(jnp.int32, (rows, rows), 1)
    allowed = (key_pos >= start) & (key_pos <= query_pos)
    return jnp.where(allowed, 0.0, MASKED)


def head_tile(q, do, k, v, k_t, bias, lse2, delta):
    scores = dot(k, q, NT)
    weights = jnp.exp2((scores * (SCALE * LOG2E) - lse2) + bias)
    weight_grads = dot(v, do, NT)
    dscore = (weights * (weight_grads - delta)).astype(jnp.bfloat16)
    half = weights.astype(jnp.bfloat16)
    return dot(k_t, dscore, NN), dot(dscore, q, NN), dot(half, do, NN)


def own_kernel(
    q_ref, do_ref, o_ref, lse_ref, len_ref, kv_ref,
    dq_ref, dkv_ref, delta_ref, start_ref, bias_ref,
):
    c = pl.program_id(0)
    rows = q_ref.shape[0]
    base = lax.axis_index("ctx") * rows

    @pl.when(c == 0)
    def _():
        pos = base + lax.broadcasted_iota(jnp.int32, (1, rows), 1)
        start = first_token(len_ref[...], pos)
        start_ref[...] = start
        bias_ref[...] = block_bias(start, rows, base, base)

    k, v = kv_ref[0], kv_ref[1]
    k_t = k.T
    dk = jnp.zeros((rows, WIDTH), jnp.float32)
    dv = jnp.zeros((rows, WIDTH), jnp.float32)
    for g in range(GROUP):
        cols = slice(g * WIDTH, (g + 1) * WIDTH)
        q, do = q_ref[:, cols], do_ref[:, cols]
        prod = do.astype(jnp.float32) * o_ref[:, cols].astype(jnp.float32)
        delta = jnp.sum(prod.T, axis=0, keepdims=True)
        head = c * GROUP + g
        delta_ref[pl.ds(head, 1), :] = delta
        lse2 = lse_ref[pl.ds(head, 1), :] * LOG2E
        dq_t, dk_h, dv_h = head_tile(q, do, k, v, k_t, bias_ref[...], lse2, delta)
        dq_ref[cols, :] = dq_t
        dk = dk + dk_h
        dv = dv + dv_h
    dkv_ref[0] = (dk * SCALE).astype(dkv_ref.dtype)
    dkv_ref[1] = dv.astype(dkv_ref.dtype)


def far_kernel(distances, final, *refs):
    count = len(distances)
    q_ref, do_ref, lse_ref, delta_ref, start_ref, acc_ref = refs[:6]
    kv_refs = refs[6 : 6 + count]
    dq_ref = refs[6 + count]
    dkv_refs = refs[7 + count : 7 + 2 * count]
    bias_ref, sum_ref = refs[7 + 2 * count :]
    c = pl.program_id(0)
    rows = q_ref.shape[0]
    base = lax.axis_index("ctx") * rows
    start = start_ref[...]
    earliest = jnp.min(start)

    sum_ref[...] = acc_ref[...]
    for n, distance in enumerate(distances):
        base_key = base - distance * rows
        live = earliest < base_key + rows

        @pl.when(live & (c == 0))
        def _():
            bias_ref[n] = block_bias(start, rows, base_key, base)

        @pl.when(live)
        def _():
            k, v = kv_refs[n][0], kv_refs[n][1]
            k_t = k.T
            dk = jnp.zeros((rows, WIDTH), jnp.float32)
            dv = jnp.zeros((rows, WIDTH), jnp.float32)
            for g in range(GROUP):
                cols = slice(g * WIDTH, (g + 1) * WIDTH)
                head = c * GROUP + g
                lse2 = lse_ref[pl.ds(head, 1), :] * LOG2E
                delta = delta_ref[pl.ds(head, 1), :]
                dq_t, dk_h, dv_h = head_tile(
                    q_ref[:, cols], do_ref[:, cols], k, v, k_t, bias_ref[n], lse2, delta
                )
                sum_ref[cols, :] += dq_t
                dk = dk + dk_h
                dv = dv + dv_h
            dkv_refs[n][0] = (dk * SCALE).astype(jnp.bfloat16)
            dkv_refs[n][1] = dv.astype(jnp.bfloat16)

        @pl.when(jnp.logical_not(live))
        def _():
            dkv_refs[n][...] = jnp.zeros(dkv_refs[n].shape, jnp.bfloat16)

    if final:
        for g in range(GROUP):
            cols = slice(g * WIDTH, (g + 1) * WIDTH)
            dq_ref[:, cols] = (sum_ref[cols, :] * SCALE).T.astype(jnp.bfloat16)
    else:
        dq_ref[...] = sum_ref[...]


def whole(shape):
    return pl.BlockSpec(shape, lambda c: (0,) * len(shape))


def specs_of(rows):
    wide = GROUP * WIDTH
    return dict(
        tokens=pl.BlockSpec((rows, wide), lambda c: (0, c)),
        acc=pl.BlockSpec((wide, rows), lambda c: (c, 0)),
        kv=pl.BlockSpec((2, rows, WIDTH), lambda c: (0, 0, c)),
        stat=whole((QUERY_HEADS, rows)),
        start=whole((1, rows)),
    )


def cost(rows, blocks):
    return pl.CostEstimate(
        flops=10 * rows * rows * WIDTH * QUERY_HEADS * blocks,
        bytes_accessed=8 * rows * QUERY_HEADS * WIDTH,
        transcendentals=rows * rows * QUERY_HEADS * blocks,
    )


def own_pass(q, do, o, lse, lengths, kv):
    rows = q.shape[0]
    s = specs_of(rows)
    return pl.pallas_call(
        own_kernel,
        grid=(KEY_VALUE_HEADS,),
        in_specs=[s["tokens"], s["tokens"], s["tokens"], s["stat"], whole(lengths.shape), s["kv"]],
        out_specs=[s["acc"], s["kv"], s["stat"], s["start"]],
        out_shape=[
            jax.ShapeDtypeStruct((QUERY_HEADS * WIDTH, rows), jnp.float32),
            jax.ShapeDtypeStruct(kv.shape, jnp.float32),
            jax.ShapeDtypeStruct((QUERY_HEADS, rows), jnp.float32),
            jax.ShapeDtypeStruct((1, rows), jnp.int32),
        ],
        scratch_shapes=[pltpu.VMEM((rows, rows), jnp.float32)],
        compiler_params=pltpu.CompilerParams(vmem_limit_bytes=32 * 2**20),
        cost_estimate=cost(rows, 1),
        name="own_block",
    )(q, do, o, lse, lengths, kv)


def far_pass(distances, final, q, do, lse, delta, start, acc, kvs):
    rows = q.shape[0]
    s = specs_of(rows)
    count = len(distances)
    if final:
        dq_spec, dq_shape = s["tokens"], jax.ShapeDtypeStruct(q.shape, jnp.bfloat16)
    else:
        dq_spec, dq_shape = s["acc"], jax.ShapeDtypeStruct(acc.shape, jnp.float32)
    return pl.pallas_call(
        functools.partial(far_kernel, distances, final),
        grid=(KEY_VALUE_HEADS,),
        in_specs=[s["tokens"], s["tokens"], s["stat"], s["stat"], s["start"], s["acc"]]
        + [s["kv"]] * count,
        out_specs=[dq_spec] + [s["kv"]] * count,
        out_shape=[dq_shape]
        + [jax.ShapeDtypeStruct(kv.shape, jnp.bfloat16) for kv in kvs],
        scratch_shapes=[
            pltpu.VMEM((count, rows, rows), jnp.float32),
            pltpu.VMEM((GROUP * WIDTH, rows), jnp.float32),
        ],
        compiler_params=pltpu.CompilerParams(vmem_limit_bytes=32 * 2**20),
        cost_estimate=cost(rows, count),
        name="far_blocks",
    )(q, do, lse, delta, start, acc, *kvs)


def per_device(queries, keys, values, outputs, grad_out, log_sums, doc_lengths):
    q, do, o, lse = queries[0], grad_out[0], outputs[0], log_sums[0]
    kv = jnp.concatenate([keys, values], axis=0)
    kv3 = around(kv, "ctx", 3)
    kv2 = around(kv, "ctx", 2)
    kv1 = around(kv, "ctx", 1)
    acc, dkv0, delta, start = own_pass(q, do, o, lse, doc_lengths, kv)
    acc, dkv3, dkv2 = far_pass((3, 2), False, q, do, lse, delta, start, acc, (kv3, kv2))
    back3 = around(dkv3, "ctx", -3)
    back2 = around(dkv2, "ctx", -2)
    dq, dkv1 = far_pass((1,), True, q, do, lse, delta, start, acc, (kv1,))
    back1 = around(dkv1, "ctx", -1)
    up_q = around(dq, "section", -1)
    total = dkv0 + back3.astype(jnp.float32) + back2.astype(jnp.float32)
    total = total + back1.astype(jnp.float32)
    up_kv = around(total.astype(jnp.bfloat16), "section", -1)
    return up_q[None], up_kv[0][None], up_kv[1][None]


def solution(mesh):
    tokens = P("section", "ctx", None)
    in_specs = (tokens,) * 5 + (P("section", None, "ctx"), P("section", None))
    return jax.shard_map(
        per_device, mesh=mesh, in_specs=in_specs, out_specs=(tokens,) * 3, check_vma=False
    )
```

```python
import functools
import math

import jax
import jax.numpy as jnp
from jax import lax
from jax.experimental import pallas as pl
from jax.experimental.pallas import tpu as pltpu
from jax.sharding import PartitionSpec as P

QUERY_HEADS = 20
KEY_VALUE_HEADS = 4
GROUP = QUERY_HEADS // KEY_VALUE_HEADS
WIDTH = 128
RING = 4
SCALE = WIDTH ** (-0.5)
LOG2E = math.log2(math.e)
MASKED = -1e30
NT = (((1,), (1,)), ((), ()))
NN = (((1,), (0,)), ((), ()))


def around(x, axis, by):
    peers = lax.axis_size(axis)
    return lax.ppermute(x, axis, [(i, (i + by) % peers) for i in range(peers)])


def dot(a, b, dims):
    return lax.dot_general(a, b, dims, preferred_element_type=jnp.float32)


def first_token(lengths, query_pos):
    docs = lengths.shape[1]
    row = lax.broadcasted_iota(jnp.int32, (docs, docs), 0)
    col = lax.broadcasted_iota(jnp.int32, (docs, docs), 1)
    ends = jnp.sum(jnp.where(col <= row, lengths, 0), axis=1, keepdims=True)
    return jnp.max(jnp.where(ends <= query_pos, ends, 0), axis=0, keepdims=True)


def block_bias(start, rows, base_key, base_query):
    key_pos = base_key + lax.broadcasted_iota(jnp.int32, (rows, rows), 0)
    query_pos = base_query + lax.broadcasted_iota(jnp.int32, (rows, rows), 1)
    allowed = (key_pos >= start) & (key_pos <= query_pos)
    return jnp.where(allowed, 0.0, MASKED)


def head_tile(q, do, k, v, k_t, bias, lse2, delta):
    scores = dot(k, q, NT)
    weights = jnp.exp2((scores * (SCALE * LOG2E) - lse2) + bias)
    weight_grads = dot(v, do, NT)
    dscore = (weights * (weight_grads - delta)).astype(jnp.bfloat16)
    half = weights.astype(jnp.bfloat16)
    return dot(k_t, dscore, NN), dot(dscore, q, NN), dot(half, do, NN)


def own_kernel(
    q_ref, do_ref, o_ref, lse_ref, len_ref, kv_ref,
    dq_ref, dkv_ref, delta_ref, start_ref, bias_ref,
):
    c = pl.program_id(0)
    rows = q_ref.shape[0]
    base = lax.axis_index("ctx") * rows

    @pl.when(c == 0)
    def _():
        pos = base + lax.broadcasted_iota(jnp.int32, (1, rows), 1)
        start = first_token(len_ref[...], pos)
        start_ref[...] = start
        bias_ref[...] = block_bias(start, rows, base, base)

    k, v = kv_ref[0], kv_ref[1]
    k_t = k.T
    dk = jnp.zeros((rows, WIDTH), jnp.float32)
    dv = jnp.zeros((rows, WIDTH), jnp.float32)
    for g in range(GROUP):
        cols = slice(g * WIDTH, (g + 1) * WIDTH)
        q, do = q_ref[:, cols], do_ref[:, cols]
        prod = do.astype(jnp.float32) * o_ref[:, cols].astype(jnp.float32)
        delta = jnp.sum(prod.T, axis=0, keepdims=True)
        head = c * GROUP + g
        delta_ref[pl.ds(head, 1), :] = delta
        lse2 = lse_ref[pl.ds(head, 1), :] * LOG2E
        dq_t, dk_h, dv_h = head_tile(q, do, k, v, k_t, bias_ref[...], lse2, delta)
        dq_ref[cols, :] = dq_t
        dk = dk + dk_h
        dv = dv + dv_h
    dkv_ref[0] = (dk * SCALE).astype(dkv_ref.dtype)
    dkv_ref[1] = dv.astype(dkv_ref.dtype)


def far_kernel(distances, final, *refs):
    count = len(distances)
    q_ref, do_ref, lse_ref, delta_ref, start_ref, acc_ref = refs[:6]
    kv_refs = refs[6 : 6 + count]
    dq_ref = refs[6 + count]
    dkv_refs = refs[7 + count : 7 + 2 * count]
    bias_ref, sum_ref = refs[7 + 2 * count :]
    c = pl.program_id(0)
    rows = q_ref.shape[0]
    base = lax.axis_index("ctx") * rows
    start = start_ref[...]
    earliest = jnp.min(start)

    sum_ref[...] = acc_ref[...]
    for n, distance in enumerate(distances):
        base_key = base - distance * rows
        live = earliest < base_key + rows

        @pl.when(live & (c == 0))
        def _():
            bias_ref[n] = block_bias(start, rows, base_key, base)

        @pl.when(live)
        def _():
            k, v = kv_refs[n][0], kv_refs[n][1]
            k_t = k.T
            dk = jnp.zeros((rows, WIDTH), jnp.float32)
            dv = jnp.zeros((rows, WIDTH), jnp.float32)
            for g in range(GROUP):
                cols = slice(g * WIDTH, (g + 1) * WIDTH)
                head = c * GROUP + g
                lse2 = lse_ref[pl.ds(head, 1), :] * LOG2E
                delta = delta_ref[pl.ds(head, 1), :]
                dq_t, dk_h, dv_h = head_tile(
                    q_ref[:, cols], do_ref[:, cols], k, v, k_t, bias_ref[n], lse2, delta
                )
                sum_ref[cols, :] += dq_t
                dk = dk + dk_h
                dv = dv + dv_h
            dkv_refs[n][0] = (dk * SCALE).astype(jnp.bfloat16)
            dkv_refs[n][1] = dv.astype(jnp.bfloat16)

        @pl.when(jnp.logical_not(live))
        def _():
            dkv_refs[n][...] = jnp.zeros(dkv_refs[n].shape, jnp.bfloat16)

    if final:
        for g in range(GROUP):
            cols = slice(g * WIDTH, (g + 1) * WIDTH)
            dq_ref[:, cols] = (sum_ref[cols, :] * SCALE).T.astype(jnp.bfloat16)
    else:
        dq_ref[...] = sum_ref[...]


def whole(shape):
    return pl.BlockSpec(shape, lambda c: (0,) * len(shape))


def specs_of(rows):
    wide = GROUP * WIDTH
    return dict(
        tokens=pl.BlockSpec((rows, wide), lambda c: (0, c)),
        acc=pl.BlockSpec((wide, rows), lambda c: (c, 0)),
        kv=pl.BlockSpec((2, rows, WIDTH), lambda c: (0, 0, c)),
        stat=whole((QUERY_HEADS, rows)),
        start=whole((1, rows)),
    )


def cost(rows, blocks):
    return pl.CostEstimate(
        flops=10 * rows * rows * WIDTH * QUERY_HEADS * blocks,
        bytes_accessed=8 * rows * QUERY_HEADS * WIDTH,
        transcendentals=rows * rows * QUERY_HEADS * blocks,
    )


def own_pass(q, do, o, lse, lengths, kv):
    rows = q.shape[0]
    s = specs_of(rows)
    return pl.pallas_call(
        own_kernel,
        grid=(KEY_VALUE_HEADS,),
        in_specs=[s["tokens"], s["tokens"], s["tokens"], s["stat"], whole(lengths.shape), s["kv"]],
        out_specs=[s["acc"], s["kv"], s["stat"], s["start"]],
        out_shape=[
            jax.ShapeDtypeStruct((QUERY_HEADS * WIDTH, rows), jnp.float32),
            jax.ShapeDtypeStruct(kv.shape, jnp.bfloat16),
            jax.ShapeDtypeStruct((QUERY_HEADS, rows), jnp.float32),
            jax.ShapeDtypeStruct((1, rows), jnp.int32),
        ],
        scratch_shapes=[pltpu.VMEM((rows, rows), jnp.float32)],
        compiler_params=pltpu.CompilerParams(vmem_limit_bytes=32 * 2**20),
        cost_estimate=cost(rows, 1),
        name="own_block",
    )(q, do, o, lse, lengths, kv)


def far_pass(distances, final, q, do, lse, delta, start, acc, kvs):
    rows = q.shape[0]
    s = specs_of(rows)
    count = len(distances)
    if final:
        dq_spec, dq_shape = s["tokens"], jax.ShapeDtypeStruct(q.shape, jnp.bfloat16)
    else:
        dq_spec, dq_shape = s["acc"], jax.ShapeDtypeStruct(acc.shape, jnp.float32)
    return pl.pallas_call(
        functools.partial(far_kernel, distances, final),
        grid=(KEY_VALUE_HEADS,),
        in_specs=[s["tokens"], s["tokens"], s["stat"], s["stat"], s["start"], s["acc"]]
        + [s["kv"]] * count,
        out_specs=[dq_spec] + [s["kv"]] * count,
        out_shape=[dq_shape]
        + [jax.ShapeDtypeStruct(kv.shape, jnp.bfloat16) for kv in kvs],
        scratch_shapes=[
            pltpu.VMEM((count, rows, rows), jnp.float32),
            pltpu.VMEM((GROUP * WIDTH, rows), jnp.float32),
        ],
        compiler_params=pltpu.CompilerParams(vmem_limit_bytes=32 * 2**20),
        cost_estimate=cost(rows, count),
        name="far_blocks",
    )(q, do, lse, delta, start, acc, *kvs)


def back_home(x, distance):
    sections, peers = lax.axis_size("section"), lax.axis_size("ctx")
    route = [
        (s * peers + i, (s - 1) % sections * peers + (i - distance) % peers)
        for s in range(sections)
        for i in range(peers)
    ]
    return lax.ppermute(x, ("section", "ctx"), route)


def after(x, *earlier):
    return lax.optimization_barrier((x, *earlier))[0]


def ring_step(x, by):
    rings = lax.axis_size("ctx") // RING
    route = [(z * RING + y, z * RING + (y + by) % RING) for z in range(rings) for y in range(RING)]
    return lax.ppermute(x, "ctx", route)


def ring_cross(x, column, by):
    rings = lax.axis_size("ctx") // RING
    route = [
        (z * RING + y, ((z + by) % rings if y == column else z) * RING + y)
        for z in range(rings)
        for y in range(RING)
    ]
    return lax.ppermute(x, "ctx", route)


def per_device(queries, keys, values, outputs, grad_out, log_sums, doc_lengths):
    q, do, o, lse = queries[0], grad_out[0], outputs[0], log_sums[0]
    f32 = jnp.float32
    kv = jnp.concatenate([keys, values], axis=0)
    kv3 = around(kv, "ctx", 3)
    near = ring_step(kv, 1)
    acc, dkv0, delta, start = own_pass(q, do, o, lse, doc_lengths, kv)
    kv1 = ring_cross(after(near, delta), 0, 1)
    kv2 = around(after(kv, kv3, near, delta), "ctx", 2)
    home0 = back_home(dkv0, 0)
    acc, dkv3 = far_pass((3,), False, q, do, lse, delta, start, acc, (kv3,))
    home3 = back_home(dkv3, 3)
    acc, dkv1 = far_pass((1,), False, q, do, lse, delta, start, acc, (kv1,))
    home1 = back_home(dkv1, 1)
    dq, dkv2 = far_pass((2,), True, q, do, lse, delta, start, acc, (kv2,))
    home2 = back_home(dkv2, 2)
    up_q = around(dq, "section", -1)
    total = home0.astype(f32) + home3.astype(f32)
    total = lax.optimization_barrier(total) + home1.astype(f32)
    total = lax.optimization_barrier(total) + home2.astype(f32)
    up_kv = total.astype(jnp.bfloat16)
    return up_q[None], up_kv[0][None], up_kv[1][None]


def solution(mesh):
    tokens = P("section", "ctx", None)
    in_specs = (tokens,) * 5 + (P("section", None, "ctx"), P("section", None))
    return jax.shard_map(
        per_device, mesh=mesh, in_specs=in_specs, out_specs=(tokens,) * 3, check_vma=False
    )
```

```python
import functools
import math

import jax
import jax.numpy as jnp
from jax import lax
from jax.experimental import pallas as pl
from jax.experimental.pallas import tpu as pltpu
from jax.sharding import PartitionSpec as P

QUERY_HEADS = 20
KEY_VALUE_HEADS = 4
GROUP = QUERY_HEADS // KEY_VALUE_HEADS
WIDTH = 128
RING = 4
SCALE = WIDTH ** (-0.5)
LOG2E = math.log2(math.e)
MASKED = -1e30
NT = (((1,), (1,)), ((), ()))
NN = (((1,), (0,)), ((), ()))


def around(x, axis, by):
    peers = lax.axis_size(axis)
    return lax.ppermute(x, axis, [(i, (i + by) % peers) for i in range(peers)])


def dot(a, b, dims):
    return lax.dot_general(a, b, dims, preferred_element_type=jnp.float32)


def first_token(lengths, query_pos):
    docs = lengths.shape[1]
    row = lax.broadcasted_iota(jnp.int32, (docs, docs), 0)
    col = lax.broadcasted_iota(jnp.int32, (docs, docs), 1)
    ends = jnp.sum(jnp.where(col <= row, lengths, 0), axis=1, keepdims=True)
    return jnp.max(jnp.where(ends <= query_pos, ends, 0), axis=0, keepdims=True)


def block_bias(start, rows, base_key, base_query):
    key_pos = base_key + lax.broadcasted_iota(jnp.int32, (rows, rows), 0)
    query_pos = base_query + lax.broadcasted_iota(jnp.int32, (rows, rows), 1)
    allowed = (key_pos >= start) & (key_pos <= query_pos)
    return jnp.where(allowed, 0.0, MASKED)


def stacked(ref):
    return jnp.concatenate([ref[:, g * WIDTH : (g + 1) * WIDTH] for g in range(GROUP)], axis=0)


def side_by_side(ref, first):
    return jnp.concatenate([ref[pl.ds(first + g, 1), :] for g in range(GROUP)], axis=1)


def group_tile(q, do, k, v, bias, lse2, delta):
    bias = jnp.concatenate([bias] * GROUP, axis=1)
    scores = dot(k, q, NT)
    weights = jnp.exp2((scores * (SCALE * LOG2E) - lse2) + bias)
    weight_grads = dot(v, do, NT)
    dscore = (weights * (weight_grads - delta)).astype(jnp.bfloat16)
    half = weights.astype(jnp.bfloat16)
    return dot(k.T, dscore, NN), dot(dscore, q, NN) * SCALE, dot(half, do, NN)


def own_kernel(
    q_ref, do_ref, o_ref, lse_ref, len_ref, kv_ref,
    dq_ref, dkv_ref, delta_ref, start_ref, bias_ref,
):
    c = pl.program_id(0)
    rows = q_ref.shape[0]
    base = lax.axis_index("ctx") * rows

    @pl.when(c == 0)
    def _():
        pos = base + lax.broadcasted_iota(jnp.int32, (1, rows), 1)
        start = first_token(len_ref[...], pos)
        start_ref[...] = start
        bias_ref[...] = block_bias(start, rows, base, base)

    first = c * GROUP
    q, do = stacked(q_ref), stacked(do_ref)
    for g in range(GROUP):
        cols = slice(g * WIDTH, (g + 1) * WIDTH)
        prod = do_ref[:, cols].astype(jnp.float32) * o_ref[:, cols].astype(jnp.float32)
        delta_ref[pl.ds(first + g, 1), :] = jnp.sum(prod.T, axis=0, keepdims=True)
    lse2 = side_by_side(lse_ref, first) * LOG2E
    delta = side_by_side(delta_ref, first)
    dq, dk, dv = group_tile(q, do, kv_ref[0], kv_ref[1], bias_ref[...], lse2, delta)
    for g in range(GROUP):
        dq_ref[g * WIDTH : (g + 1) * WIDTH, :] = dq[:, g * rows : (g + 1) * rows]
    dkv_ref[0] = dk.astype(dkv_ref.dtype)
    dkv_ref[1] = dv.astype(dkv_ref.dtype)


def far_kernel(distances, final, *refs):
    count = len(distances)
    q_ref, do_ref, lse_ref, delta_ref, start_ref, acc_ref = refs[:6]
    kv_refs = refs[6 : 6 + count]
    dq_ref = refs[6 + count]
    dkv_refs = refs[7 + count : 7 + 2 * count]
    bias_ref, sum_ref = refs[7 + 2 * count :]
    c = pl.program_id(0)
    rows = q_ref.shape[0]
    base = lax.axis_index("ctx") * rows
    start = start_ref[...]
    earliest = jnp.min(start)

    sum_ref[...] = acc_ref[...]
    for n, distance in enumerate(distances):
        base_key = base - distance * rows
        live = earliest < base_key + rows

        @pl.when(live & (c == 0))
        def _():
            bias_ref[n] = block_bias(start, rows, base_key, base)

        @pl.when(live)
        def _():
            first = c * GROUP
            lse2 = side_by_side(lse_ref, first) * LOG2E
            delta = side_by_side(delta_ref, first)
            dq, dk, dv = group_tile(
                stacked(q_ref), stacked(do_ref), kv_refs[n][0], kv_refs[n][1], bias_ref[n], lse2, delta
            )
            for g in range(GROUP):
                sum_ref[g * WIDTH : (g + 1) * WIDTH, :] += dq[:, g * rows : (g + 1) * rows]
            dkv_refs[n][0] = dk.astype(jnp.bfloat16)
            dkv_refs[n][1] = dv.astype(jnp.bfloat16)

        @pl.when(jnp.logical_not(live))
        def _():
            dkv_refs[n][...] = jnp.zeros(dkv_refs[n].shape, jnp.bfloat16)

    if final:
        for g in range(GROUP):
            cols = slice(g * WIDTH, (g + 1) * WIDTH)
            dq_ref[:, cols] = (sum_ref[cols, :] * SCALE).T.astype(jnp.bfloat16)
    else:
        dq_ref[...] = sum_ref[...]


def whole(shape):
    return pl.BlockSpec(shape, lambda c: (0,) * len(shape))


def specs_of(rows):
    wide = GROUP * WIDTH
    return dict(
        tokens=pl.BlockSpec((rows, wide), lambda c: (0, c)),
        acc=pl.BlockSpec((wide, rows), lambda c: (c, 0)),
        kv=pl.BlockSpec((2, rows, WIDTH), lambda c: (0, 0, c)),
        stat=whole((QUERY_HEADS, rows)),
        start=whole((1, rows)),
    )


def cost(rows, blocks):
    return pl.CostEstimate(
        flops=10 * rows * rows * WIDTH * QUERY_HEADS * blocks,
        bytes_accessed=8 * rows * QUERY_HEADS * WIDTH,
        transcendentals=rows * rows * QUERY_HEADS * blocks,
    )


def own_pass(q, do, o, lse, lengths, kv):
    rows = q.shape[0]
    s = specs_of(rows)
    return pl.pallas_call(
        own_kernel,
        grid=(KEY_VALUE_HEADS,),
        in_specs=[s["tokens"], s["tokens"], s["tokens"], s["stat"], whole(lengths.shape), s["kv"]],
        out_specs=[s["acc"], s["kv"], s["stat"], s["start"]],
        out_shape=[
            jax.ShapeDtypeStruct((QUERY_HEADS * WIDTH, rows), jnp.float32),
            jax.ShapeDtypeStruct(kv.shape, jnp.bfloat16),
            jax.ShapeDtypeStruct((QUERY_HEADS, rows), jnp.float32),
            jax.ShapeDtypeStruct((1, rows), jnp.int32),
        ],
        scratch_shapes=[pltpu.VMEM((rows, rows), jnp.float32)],
        compiler_params=pltpu.CompilerParams(vmem_limit_bytes=32 * 2**20),
        cost_estimate=cost(rows, 1),
        name="own_block",
    )(q, do, o, lse, lengths, kv)


def far_pass(distances, final, q, do, lse, delta, start, acc, kvs):
    rows = q.shape[0]
    s = specs_of(rows)
    count = len(distances)
    if final:
        dq_spec, dq_shape = s["tokens"], jax.ShapeDtypeStruct(q.shape, jnp.bfloat16)
    else:
        dq_spec, dq_shape = s["acc"], jax.ShapeDtypeStruct(acc.shape, jnp.float32)
    return pl.pallas_call(
        functools.partial(far_kernel, distances, final),
        grid=(KEY_VALUE_HEADS,),
        in_specs=[s["tokens"], s["tokens"], s["stat"], s["stat"], s["start"], s["acc"]]
        + [s["kv"]] * count,
        out_specs=[dq_spec] + [s["kv"]] * count,
        out_shape=[dq_shape]
        + [jax.ShapeDtypeStruct(kv.shape, jnp.bfloat16) for kv in kvs],
        scratch_shapes=[
            pltpu.VMEM((count, rows, rows), jnp.float32),
            pltpu.VMEM((GROUP * WIDTH, rows), jnp.float32),
        ],
        compiler_params=pltpu.CompilerParams(vmem_limit_bytes=32 * 2**20),
        cost_estimate=cost(rows, count),
        name="far_blocks",
    )(q, do, lse, delta, start, acc, *kvs)


def back_home(x, distance):
    sections, peers = lax.axis_size("section"), lax.axis_size("ctx")
    route = [
        (s * peers + i, (s - 1) % sections * peers + (i - distance) % peers)
        for s in range(sections)
        for i in range(peers)
    ]
    return lax.ppermute(x, ("section", "ctx"), route)


def after(x, *earlier):
    return lax.optimization_barrier((x, *earlier))[0]


def ring_step(x, by):
    rings = lax.axis_size("ctx") // RING
    route = [(z * RING + y, z * RING + (y + by) % RING) for z in range(rings) for y in range(RING)]
    return lax.ppermute(x, "ctx", route)


def ring_across(x, column, by):
    rings = lax.axis_size("ctx") // RING
    route = [
        (z * RING + y, ((z + by) % rings if y != column else z) * RING + y)
        for z in range(rings)
        for y in range(RING)
    ]
    return lax.ppermute(x, "ctx", route)


def ring_cross(x, column, by):
    rings = lax.axis_size("ctx") // RING
    route = [
        (z * RING + y, ((z + by) % rings if y == column else z) * RING + y)
        for z in range(rings)
        for y in range(RING)
    ]
    return lax.ppermute(x, "ctx", route)


def per_device(queries, keys, values, outputs, grad_out, log_sums, doc_lengths):
    q, do, o, lse = queries[0], grad_out[0], outputs[0], log_sums[0]
    f32 = jnp.float32
    kv = jnp.concatenate([keys, values], axis=0)
    kv1 = around(kv, "ctx", 1)
    turn = ring_step(kv, -1)
    acc, dkv0, delta, start = own_pass(q, do, o, lse, doc_lengths, kv)
    kv2 = around(after(kv, delta), "ctx", 2)
    kv3 = ring_across(after(turn, delta), RING - 1, 1)
    home0 = back_home(dkv0, 0)
    acc, dkv1 = far_pass((1,), False, q, do, lse, delta, start, acc, (kv1,))
    home1 = back_home(dkv1, 1)
    acc, dkv2 = far_pass((2,), False, q, do, lse, delta, start, acc, (kv2,))
    home2 = back_home(dkv2, 2)
    dq, dkv3 = far_pass((3,), True, q, do, lse, delta, start, acc, (kv3,))
    home3 = back_home(dkv3, 3)
    up_q = around(dq, "section", -1)
    total = home0.astype(f32) + home1.astype(f32)
    total = lax.optimization_barrier(total) + home2.astype(f32)
    total = lax.optimization_barrier(total) + home3.astype(f32)
    up_kv = total.astype(jnp.bfloat16)
    return up_q[None], up_kv[0][None], up_kv[1][None]


def solution(mesh):
    tokens = P("section", "ctx", None)
    in_specs = (tokens,) * 5 + (P("section", None, "ctx"), P("section", None))
    return jax.shard_map(
        per_device, mesh=mesh, in_specs=in_specs, out_specs=(tokens,) * 3, check_vma=False
    )
```

```python
import functools
import math

import jax
import jax.numpy as jnp
from jax import lax
from jax.experimental import pallas as pl
from jax.experimental.pallas import tpu as pltpu
from jax.sharding import PartitionSpec as P

QUERY_HEADS = 20
KEY_VALUE_HEADS = 4
GROUP = QUERY_HEADS // KEY_VALUE_HEADS
WIDTH = 128
RING = 4
SCALE = WIDTH ** (-0.5)
LOG2E = math.log2(math.e)
MASKED = -1e30
NT = (((1,), (1,)), ((), ()))
NN = (((1,), (0,)), ((), ()))


def around(x, axis, by):
    peers = lax.axis_size(axis)
    return lax.ppermute(x, axis, [(i, (i + by) % peers) for i in range(peers)])


def dot(a, b, dims):
    return lax.dot_general(a, b, dims, preferred_element_type=jnp.float32)


def first_token(lengths, query_pos):
    docs = lengths.shape[1]
    row = lax.broadcasted_iota(jnp.int32, (docs, docs), 0)
    col = lax.broadcasted_iota(jnp.int32, (docs, docs), 1)
    ends = jnp.sum(jnp.where(col <= row, lengths, 0), axis=1, keepdims=True)
    return jnp.max(jnp.where(ends <= query_pos, ends, 0), axis=0, keepdims=True)


def block_bias(start, rows, base_key, base_query):
    key_pos = base_key + lax.broadcasted_iota(jnp.int32, (rows, rows), 0)
    query_pos = base_query + lax.broadcasted_iota(jnp.int32, (rows, rows), 1)
    allowed = (key_pos >= start) & (key_pos <= query_pos)
    return jnp.where(allowed, 0.0, MASKED)


def stacked(ref):
    return jnp.concatenate([ref[:, g * WIDTH : (g + 1) * WIDTH] for g in range(GROUP)], axis=0)


def side_by_side(ref, first):
    return jnp.concatenate([ref[pl.ds(first + g, 1), :] for g in range(GROUP)], axis=1)


def group_tile(q, do, k, v, bias, lse2, delta):
    bias = jnp.concatenate([bias] * GROUP, axis=1)
    scores = dot(k, q, NT)
    weights = jnp.exp2((scores * (SCALE * LOG2E) - lse2) + bias)
    weight_grads = dot(v, do, NT)
    dscore = (weights * (weight_grads - delta)).astype(jnp.bfloat16)
    half = weights.astype(jnp.bfloat16)
    return dot(k.T, dscore, NN), dot(dscore, q, NN) * SCALE, dot(half, do, NN)


def own_kernel(
    q_ref, do_ref, o_ref, lse_ref, len_ref, kv_ref,
    dq_ref, dkv_ref, delta_ref, start_ref, bias_ref,
):
    c = pl.program_id(0)
    rows = q_ref.shape[0]
    base = lax.axis_index("ctx") * rows

    @pl.when(c == 0)
    def _():
        pos = base + lax.broadcasted_iota(jnp.int32, (1, rows), 1)
        start = first_token(len_ref[...], pos)
        start_ref[...] = start
        bias_ref[...] = block_bias(start, rows, base, base)

    first = c * GROUP
    q, do = stacked(q_ref), stacked(do_ref)
    for g in range(GROUP):
        cols = slice(g * WIDTH, (g + 1) * WIDTH)
        prod = do_ref[:, cols].astype(jnp.float32) * o_ref[:, cols].astype(jnp.float32)
        delta_ref[pl.ds(first + g, 1), :] = jnp.sum(prod.T, axis=0, keepdims=True)
    lse2 = side_by_side(lse_ref, first) * LOG2E
    delta = side_by_side(delta_ref, first)
    dq, dk, dv = group_tile(q, do, kv_ref[0], kv_ref[1], bias_ref[...], lse2, delta)
    for g in range(GROUP):
        dq_ref[g * WIDTH : (g + 1) * WIDTH, :] = dq[:, g * rows : (g + 1) * rows]
    dkv_ref[0] = dk.astype(dkv_ref.dtype)
    dkv_ref[1] = dv.astype(dkv_ref.dtype)


def far_kernel(distance, final, *refs):
    q_ref, do_ref, lse_ref, delta_ref, start_ref, acc_ref, kv_ref = refs[:7]
    dq_ref, dkv_ref, bias_ref = refs[7:]
    c = pl.program_id(0)
    rows = q_ref.shape[0]
    base = lax.axis_index("ctx") * rows
    base_key = base - distance * rows
    start = start_ref[...]
    live = jnp.min(start) < base_key + rows

    def put(g, total):
        part = slice(g * WIDTH, (g + 1) * WIDTH)
        if final:
            dq_ref[:, part] = (total * SCALE).T.astype(jnp.bfloat16)
        else:
            dq_ref[part, :] = total

    def accumulated(g):
        return acc_ref[g * WIDTH : (g + 1) * WIDTH, :]

    @pl.when(live & (c == 0))
    def _():
        bias_ref[...] = block_bias(start, rows, base_key, base)

    @pl.when(live)
    def _():
        first = c * GROUP
        lse2 = side_by_side(lse_ref, first) * LOG2E
        delta = side_by_side(delta_ref, first)
        dq, dk, dv = group_tile(
            stacked(q_ref), stacked(do_ref), kv_ref[0], kv_ref[1], bias_ref[...], lse2, delta
        )
        for g in range(GROUP):
            put(g, accumulated(g) + dq[:, g * rows : (g + 1) * rows])
        dkv_ref[0] = dk.astype(jnp.bfloat16)
        dkv_ref[1] = dv.astype(jnp.bfloat16)

    @pl.when(jnp.logical_not(live))
    def _():
        for g in range(GROUP):
            put(g, accumulated(g))
        dkv_ref[...] = jnp.zeros(dkv_ref.shape, jnp.bfloat16)


def whole(shape):
    return pl.BlockSpec(shape, lambda c: (0,) * len(shape))


def specs_of(rows):
    wide = GROUP * WIDTH
    return dict(
        tokens=pl.BlockSpec((rows, wide), lambda c: (0, c)),
        acc=pl.BlockSpec((wide, rows), lambda c: (c, 0)),
        kv=pl.BlockSpec((2, rows, WIDTH), lambda c: (0, 0, c)),
        stat=whole((QUERY_HEADS, rows)),
        start=whole((1, rows)),
    )


def cost(rows, blocks):
    return pl.CostEstimate(
        flops=10 * rows * rows * WIDTH * QUERY_HEADS * blocks,
        bytes_accessed=8 * rows * QUERY_HEADS * WIDTH,
        transcendentals=rows * rows * QUERY_HEADS * blocks,
    )


def own_pass(q, do, o, lse, lengths, kv):
    rows = q.shape[0]
    s = specs_of(rows)
    return pl.pallas_call(
        own_kernel,
        grid=(KEY_VALUE_HEADS,),
        in_specs=[s["tokens"], s["tokens"], s["tokens"], s["stat"], whole(lengths.shape), s["kv"]],
        out_specs=[s["acc"], s["kv"], s["stat"], s["start"]],
        out_shape=[
            jax.ShapeDtypeStruct((QUERY_HEADS * WIDTH, rows), jnp.float32),
            jax.ShapeDtypeStruct(kv.shape, jnp.bfloat16),
            jax.ShapeDtypeStruct((QUERY_HEADS, rows), jnp.float32),
            jax.ShapeDtypeStruct((1, rows), jnp.int32),
        ],
        scratch_shapes=[pltpu.VMEM((rows, rows), jnp.float32)],
        compiler_params=pltpu.CompilerParams(vmem_limit_bytes=32 * 2**20),
        cost_estimate=cost(rows, 1),
        name="own_block",
    )(q, do, o, lse, lengths, kv)


def far_pass(distance, final, q, do, lse, delta, start, acc, kv):
    rows = q.shape[0]
    s = specs_of(rows)
    if final:
        dq_spec, dq_shape = s["tokens"], jax.ShapeDtypeStruct(q.shape, jnp.bfloat16)
    else:
        dq_spec, dq_shape = s["acc"], jax.ShapeDtypeStruct(acc.shape, jnp.float32)
    return pl.pallas_call(
        functools.partial(far_kernel, distance, final),
        grid=(KEY_VALUE_HEADS,),
        in_specs=[s["tokens"], s["tokens"], s["stat"], s["stat"], s["start"], s["acc"], s["kv"]],
        out_specs=[dq_spec, s["kv"]],
        out_shape=[dq_shape, jax.ShapeDtypeStruct(kv.shape, jnp.bfloat16)],
        scratch_shapes=[pltpu.VMEM((rows, rows), jnp.float32)],
        compiler_params=pltpu.CompilerParams(vmem_limit_bytes=32 * 2**20),
        cost_estimate=cost(rows, 1),
        name="far_block",
    )(q, do, lse, delta, start, acc, kv)


def back_home(x, distance):
    sections, peers = lax.axis_size("section"), lax.axis_size("ctx")
    route = [
        (s * peers + i, (s - 1) % sections * peers + (i - distance) % peers)
        for s in range(sections)
        for i in range(peers)
    ]
    return lax.ppermute(x, ("section", "ctx"), route)


def after(x, *earlier):
    return lax.optimization_barrier((x, *earlier))[0]


def ring_step(x, by):
    rings = lax.axis_size("ctx") // RING
    route = [(z * RING + y, z * RING + (y + by) % RING) for z in range(rings) for y in range(RING)]
    return lax.ppermute(x, "ctx", route)


def ring_across(x, column, by):
    rings = lax.axis_size("ctx") // RING
    route = [
        (z * RING + y, ((z + by) % rings if y != column else z) * RING + y)
        for z in range(rings)
        for y in range(RING)
    ]
    return lax.ppermute(x, "ctx", route)


def per_device(queries, keys, values, outputs, grad_out, log_sums, doc_lengths):
    q, do, o, lse = queries[0], grad_out[0], outputs[0], log_sums[0]
    f32 = jnp.float32
    kv = jnp.concatenate([keys, values], axis=0)
    kv1 = around(kv, "ctx", 1)
    turn = ring_step(kv, -1)
    acc, dkv0, delta, start = own_pass(q, do, o, lse, doc_lengths, kv)
    kv2 = around(after(kv, delta, turn), "ctx", 2)
    kv3 = ring_across(after(turn, delta), RING - 1, 1)
    home0 = back_home(dkv0, 0)
    acc, dkv1 = far_pass(1, False, q, do, lse, delta, start, acc, kv1)
    home1 = back_home(dkv1, 1)
    acc, dkv2 = far_pass(2, False, q, do, lse, delta, start, acc, kv2)
    home2 = back_home(dkv2, 2)
    dq, dkv3 = far_pass(3, True, q, do, lse, delta, start, acc, kv3)
    home3 = back_home(dkv3, 3)
    up_q = around(dq, "section", -1)
    total = home0.astype(f32) + home1.astype(f32)
    total = lax.optimization_barrier(total) + home2.astype(f32)
    total = lax.optimization_barrier(total) + home3.astype(f32)
    up_kv = total.astype(jnp.bfloat16)
    return up_q[None], up_kv[0][None], up_kv[1][None]


def solution(mesh):
    tokens = P("section", "ctx", None)
    in_specs = (tokens,) * 5 + (P("section", None, "ctx"), P("section", None))
    return jax.shard_map(
        per_device, mesh=mesh, in_specs=in_specs, out_specs=(tokens,) * 3, check_vma=False
    )
```

```python
import functools
import math

import jax
import jax.numpy as jnp
from jax import lax
from jax.experimental import pallas as pl
from jax.experimental.pallas import tpu as pltpu
from jax.sharding import PartitionSpec as P

QUERY_HEADS = 20
KEY_VALUE_HEADS = 4
GROUP = QUERY_HEADS // KEY_VALUE_HEADS
WIDTH = 128
RING = 4
SCALE = WIDTH ** (-0.5)
LOG2E = math.log2(math.e)
MASKED = -1e30
NT = (((1,), (1,)), ((), ()))
NN = (((1,), (0,)), ((), ()))


def around(x, axis, by):
    peers = lax.axis_size(axis)
    return lax.ppermute(x, axis, [(i, (i + by) % peers) for i in range(peers)])


def dot(a, b, dims):
    return lax.dot_general(a, b, dims, preferred_element_type=jnp.float32)


def first_token(lengths, query_pos):
    docs = lengths.shape[1]
    row = lax.broadcasted_iota(jnp.int32, (docs, docs), 0)
    col = lax.broadcasted_iota(jnp.int32, (docs, docs), 1)
    ends = jnp.sum(jnp.where(col <= row, lengths, 0), axis=1, keepdims=True)
    return jnp.max(jnp.where(ends <= query_pos, ends, 0), axis=0, keepdims=True)


def block_bias(start, rows, base_key, base_query):
    key_pos = base_key + lax.broadcasted_iota(jnp.int32, (rows, rows), 0)
    query_pos = base_query + lax.broadcasted_iota(jnp.int32, (rows, rows), 1)
    allowed = (key_pos >= start) & (key_pos <= query_pos)
    return jnp.where(allowed, 0.0, MASKED)


def stacked(ref):
    return jnp.concatenate([ref[:, g * WIDTH : (g + 1) * WIDTH] for g in range(GROUP)], axis=0)


def side_by_side(ref, first):
    return jnp.concatenate([ref[pl.ds(first + g, 1), :] for g in range(GROUP)], axis=1)


def group_tile(q, do, k, v, bias, lse2, delta):
    bias = jnp.concatenate([bias] * GROUP, axis=1)
    scores = dot(k, q, NT)
    weights = jnp.exp2((scores * (SCALE * LOG2E) - lse2) + bias)
    weight_grads = dot(v, do, NT)
    dscore = (weights * (weight_grads - delta)).astype(jnp.bfloat16)
    half = weights.astype(jnp.bfloat16)
    return dot(k.T, dscore, NN), dot(dscore, q, NN) * SCALE, dot(half, do, NN)


def own_kernel(
    q_ref, do_ref, o_ref, lse_ref, len_ref, kv_ref,
    dq_ref, dkv_ref, delta_ref, start_ref, bias_ref,
):
    c = pl.program_id(0)
    rows = q_ref.shape[0]
    base = lax.axis_index("ctx") * rows

    @pl.when(c == 0)
    def _():
        pos = base + lax.broadcasted_iota(jnp.int32, (1, rows), 1)
        start = first_token(len_ref[...], pos)
        start_ref[...] = start
        bias_ref[...] = block_bias(start, rows, base, base)

    first = c * GROUP
    q, do = stacked(q_ref), stacked(do_ref)
    for g in range(GROUP):
        cols = slice(g * WIDTH, (g + 1) * WIDTH)
        prod = do_ref[:, cols].astype(jnp.float32) * o_ref[:, cols].astype(jnp.float32)
        delta_ref[pl.ds(first + g, 1), :] = jnp.sum(prod.T, axis=0, keepdims=True)
    lse2 = side_by_side(lse_ref, first) * LOG2E
    delta = side_by_side(delta_ref, first)
    dq, dk, dv = group_tile(q, do, kv_ref[0], kv_ref[1], bias_ref[...], lse2, delta)
    for g in range(GROUP):
        dq_ref[g * WIDTH : (g + 1) * WIDTH, :] = dq[:, g * rows : (g + 1) * rows]
    dkv_ref[0] = dk.astype(dkv_ref.dtype)
    dkv_ref[1] = dv.astype(dkv_ref.dtype)


def far_kernel(distance, final, *refs):
    q_ref, do_ref, lse_ref, delta_ref, start_ref, acc_ref, kv_ref = refs[:7]
    dq_ref, dkv_ref, bias_ref = refs[7:]
    c = pl.program_id(0)
    rows = q_ref.shape[0]
    base = lax.axis_index("ctx") * rows
    base_key = base - distance * rows
    start = start_ref[...]
    live = jnp.min(start) < base_key + rows

    def put(g, total):
        part = slice(g * WIDTH, (g + 1) * WIDTH)
        if final:
            dq_ref[:, part] = (total * SCALE).astype(jnp.bfloat16).T
        else:
            dq_ref[part, :] = total

    def accumulated(g):
        return acc_ref[g * WIDTH : (g + 1) * WIDTH, :]

    @pl.when(live & (c == 0))
    def _():
        bias_ref[...] = block_bias(start, rows, base_key, base)

    @pl.when(live)
    def _():
        first = c * GROUP
        lse2 = side_by_side(lse_ref, first) * LOG2E
        delta = side_by_side(delta_ref, first)
        dq, dk, dv = group_tile(
            stacked(q_ref), stacked(do_ref), kv_ref[0], kv_ref[1], bias_ref[...], lse2, delta
        )
        for g in range(GROUP):
            put(g, accumulated(g) + dq[:, g * rows : (g + 1) * rows])
        dkv_ref[0] = dk.astype(jnp.bfloat16)
        dkv_ref[1] = dv.astype(jnp.bfloat16)

    @pl.when(jnp.logical_not(live))
    def _():
        for g in range(GROUP):
            put(g, accumulated(g))
        dkv_ref[...] = jnp.zeros(dkv_ref.shape, jnp.bfloat16)


def whole(shape):
    return pl.BlockSpec(shape, lambda c: (0,) * len(shape))


def specs_of(rows):
    wide = GROUP * WIDTH
    return dict(
        tokens=pl.BlockSpec((rows, wide), lambda c: (0, c)),
        acc=pl.BlockSpec((wide, rows), lambda c: (c, 0)),
        kv=pl.BlockSpec((2, rows, WIDTH), lambda c: (0, 0, c)),
        stat=whole((QUERY_HEADS, rows)),
        start=whole((1, rows)),
    )


def cost(rows, blocks):
    return pl.CostEstimate(
        flops=10 * rows * rows * WIDTH * QUERY_HEADS * blocks,
        bytes_accessed=8 * rows * QUERY_HEADS * WIDTH,
        transcendentals=rows * rows * QUERY_HEADS * blocks,
    )


def own_pass(q, do, o, lse, lengths, kv):
    rows = q.shape[0]
    s = specs_of(rows)
    return pl.pallas_call(
        own_kernel,
        grid=(KEY_VALUE_HEADS,),
        in_specs=[s["tokens"], s["tokens"], s["tokens"], s["stat"], whole(lengths.shape), s["kv"]],
        out_specs=[s["acc"], s["kv"], s["stat"], s["start"]],
        out_shape=[
            jax.ShapeDtypeStruct((QUERY_HEADS * WIDTH, rows), jnp.float32),
            jax.ShapeDtypeStruct(kv.shape, jnp.bfloat16),
            jax.ShapeDtypeStruct((QUERY_HEADS, rows), jnp.float32),
            jax.ShapeDtypeStruct((1, rows), jnp.int32),
        ],
        scratch_shapes=[pltpu.VMEM((rows, rows), jnp.float32)],
        compiler_params=pltpu.CompilerParams(vmem_limit_bytes=32 * 2**20),
        cost_estimate=cost(rows, 1),
        name="own_block",
    )(q, do, o, lse, lengths, kv)


def far_pass(distance, final, q, do, lse, delta, start, acc, kv):
    rows = q.shape[0]
    s = specs_of(rows)
    if final:
        dq_spec, dq_shape = s["tokens"], jax.ShapeDtypeStruct(q.shape, jnp.bfloat16)
    else:
        dq_spec, dq_shape = s["acc"], jax.ShapeDtypeStruct(acc.shape, jnp.float32)
    return pl.pallas_call(
        functools.partial(far_kernel, distance, final),
        grid=(KEY_VALUE_HEADS,),
        in_specs=[s["tokens"], s["tokens"], s["stat"], s["stat"], s["start"], s["acc"], s["kv"]],
        out_specs=[dq_spec, s["kv"]],
        out_shape=[dq_shape, jax.ShapeDtypeStruct(kv.shape, jnp.bfloat16)],
        scratch_shapes=[pltpu.VMEM((rows, rows), jnp.float32)],
        compiler_params=pltpu.CompilerParams(vmem_limit_bytes=32 * 2**20),
        cost_estimate=cost(rows, 1),
        name="far_block",
    )(q, do, lse, delta, start, acc, kv)


def back_home(x, distance):
    sections, peers = lax.axis_size("section"), lax.axis_size("ctx")
    route = [
        (s * peers + i, (s - 1) % sections * peers + (i - distance) % peers)
        for s in range(sections)
        for i in range(peers)
    ]
    return lax.ppermute(x, ("section", "ctx"), route)


def after(x, *earlier):
    return lax.optimization_barrier((x, *earlier))[0]


def ring_step(x, by):
    rings = lax.axis_size("ctx") // RING
    route = [(z * RING + y, z * RING + (y + by) % RING) for z in range(rings) for y in range(RING)]
    return lax.ppermute(x, "ctx", route)


def ring_across(x, column, by):
    rings = lax.axis_size("ctx") // RING
    route = [
        (z * RING + y, ((z + by) % rings if y != column else z) * RING + y)
        for z in range(rings)
        for y in range(RING)
    ]
    return lax.ppermute(x, "ctx", route)


def per_device(queries, keys, values, outputs, grad_out, log_sums, doc_lengths):
    q, do, o, lse = queries[0], grad_out[0], outputs[0], log_sums[0]
    f32 = jnp.float32
    kv = jnp.concatenate([keys, values], axis=0)
    kv1 = around(kv, "ctx", 1)
    turn = ring_step(kv, -1)
    acc, dkv0, delta, start = own_pass(q, do, o, lse, doc_lengths, kv)
    kv2 = around(after(kv, delta, turn), "ctx", 2)
    kv3 = ring_across(after(turn, delta), RING - 1, 1)
    home0 = back_home(dkv0, 0)
    acc, dkv1 = far_pass(1, False, q, do, lse, delta, start, acc, kv1)
    home1 = back_home(dkv1, 1)
    acc, dkv2 = far_pass(2, False, q, do, lse, delta, start, acc, kv2)
    home2 = back_home(dkv2, 2)
    dq, dkv3 = far_pass(3, True, q, do, lse, delta, start, acc, kv3)
    home3 = back_home(dkv3, 3)
    up_q = around(dq, "section", -1)
    total = home0.astype(f32) + home1.astype(f32)
    total = lax.optimization_barrier(total) + home2.astype(f32)
    total = lax.optimization_barrier(total) + home3.astype(f32)
    up_kv = total.astype(jnp.bfloat16)
    return up_q[None], up_kv[0][None], up_kv[1][None]


def solution(mesh):
    tokens = P("section", "ctx", None)
    in_specs = (tokens,) * 5 + (P("section", None, "ctx"), P("section", None))
    return jax.shard_map(
        per_device, mesh=mesh, in_specs=in_specs, out_specs=(tokens,) * 3, check_vma=False
    )
```
